32 devices in a mesh: gx: 4 (over z), gy: 8 (over y, x, core).
Axes of the slice: x: 2, y: 2, z: 4, core: 2. Of those that a mesh axis runs over, the one named last changes fastest.
Arguments:
- enthalpy: float32 [64, 128, 1024], P(None, 'gx', 'gy'), may hold values from -6 to 6
- heat_cap: float32 [64, 128, 1024], P(None, 'gx', 'gy'), may hold values from 1 to 2
- conductivity: float32 [64, 128, 1024], P(None, 'gx', 'gy'), may hold values from 0.5 to 2
- phase: int32 [64, 128, 1024], P(None, 'gx', 'gy'), may hold values 0 or 1
- level_set: float32 [64, 128, 1024], P(None, 'gx', 'gy'), may hold values from -6 to 6
- band_flag: int32 [2, 4, 32], P(None, 'gx', 'gy'), may hold values from 0 to 1, as said below
Outputs:
- enthalpy_out: float32 [64, 128, 1024], P(None, 'gx', 'gy')
- level_out: float32 [64, 128, 1024], P(None, 'gx', 'gy')
The draws below stay inside these ranges and needn't reach their ends.
Inputs may be any that keep to these rules, and one draw needn't show every extreme that they name: `band_flag`: two devices whose gy indices differ only in the lowest bit hold together exactly 4 band tiles among their tiles; for each gx index, at least one pair of gy indices (2k, 2k+1) has one device holding all 4 band tiles and its partner none.
All inputs are finite; a program needn't handle non-finite values. No bound on the sum of `phase` on one device may be relied on, other than what follows from the above.
Results may differ from the reference program's by a relative error of at most 0.0003.
Values sent between devices are 32-bit elements; how exact they have to be, the bound alone decides.
A program may use at most 128 MiB of HBM per device.

```python
import math
import jax
import jax.numpy as jnp
from jax import lax

NZ = 64
TILE = 32
CX = 32
CY = 128
NX = 128
NY = 1024
N_GX = 4
N_GY = 8


def draw_band_flag(key, part):
    tiles_z = NZ // TILE
    tiles_x = CX // TILE
    tiles_y = CY // TILE
    tiles_all = tiles_z * tiles_x * tiles_y
    quarter = tiles_all // 4
    pair_total = N_GY // 2
    key_first = jax.random.fold_in(key, 11)
    key_chosen = jax.random.fold_in(key, 12)
    key_extreme = jax.random.fold_in(key, 13)
    key_order = jax.random.fold_in(key, 14)
    first_counts = jax.random.randint(key_first, (N_GX, pair_total), 0, 2 * quarter + 1)
    chosen_pair = jax.random.randint(key_chosen, (N_GX,), 0, pair_total)
    extreme = jax.random.randint(key_extreme, (N_GX,), 0, 2) * (2 * quarter)
    pair_ids = jnp.arange(pair_total, dtype=jnp.int32)
    first_counts = jnp.where(pair_ids[None, :] == chosen_pair[:, None], extreme[:, None], first_counts)
    counts = jnp.stack([first_counts, 2 * quarter - first_counts], -1).reshape(N_GX * N_GY)
    order_keys = jax.random.split(key_order, N_GX * N_GY)
    orders = jax.vmap(lambda single: jax.random.permutation(single, tiles_all))(order_keys)
    flags = (orders < counts[:, None]).astype(jnp.int32)
    flags = flags.reshape(N_GX, N_GY, tiles_z, tiles_x, tiles_y)
    flags = jnp.transpose(flags, (2, 0, 3, 1, 4))
    return flags.reshape(tiles_z, N_GX * tiles_x, N_GY * tiles_y)


def set_ends(drawn, stream_key, smallest, largest):
    longest = drawn.shape.index(max(drawn.shape))
    spots = []
    for shift in (0, 1):
        where = [jax.random.randint(jax.random.fold_in(stream_key, axis), (), 0, length) for axis, length in enumerate(drawn.shape)]
        where[longest] = (where[longest] + shift) % drawn.shape[longest]
        spots.append(tuple(where))
    return drawn.at[spots[0]].set(smallest).at[spots[1]].set(largest)


def block_scale(key, dims, cuts, low, largest):
    level = 1.0
    for position, shards_of in cuts:
        draws = jax.random.uniform(jax.random.fold_in(jax.random.fold_in(key, 6), position), (shards_of,), jnp.float32, low / len(cuts), largest / len(cuts))
        level = level * jnp.repeat(jnp.exp(draws), dims[position] // shards_of).reshape((-1,) + (1,) * (len(dims) - 1 - position))
    return level


def gaussian(stream_key, dims, scale, most, pieces=(), kind=jnp.bfloat16):
    result = jax.random.normal(stream_key, dims, jnp.float32) * scale
    if len(pieces) > 0:
        result = block_scale(stream_key, dims, pieces, -0.22, 0.18) * result
    return jnp.clip(result, min=-most, max=most).astype(kind)


def setup_inputs(seed: int = 0) -> dict:
    streams_of = jax.random.split(jax.random.key(seed), 7)
    enthalpy = gaussian(streams_of[0], (NZ, NX, NY), 1.0, 6.0, ((1, 4), (2, 8)), jnp.float32)
    heat_cap = jnp.clip(jnp.exp(math.log(2.0) - 0.6931472 * jax.random.uniform(streams_of[1], (NZ, NX, NY), jnp.float32) ** block_scale(streams_of[1], (NZ, NX, NY), ((1, 4), (2, 8)), -0.2, 0.2)), 1.0, 2.0)
    conductivity = jnp.clip(jnp.exp(math.log(2.0) - 1.3862944 * jax.random.uniform(streams_of[2], (NZ, NX, NY), jnp.float32) ** block_scale(streams_of[2], (NZ, NX, NY), ((1, 4), (2, 8)), -0.2, 0.2)), 0.5, 2.0)
    phase = set_ends((jax.random.randint(streams_of[3], (NZ, NX, NY), 0, 2) < 1).astype(jnp.int32), jax.random.fold_in(streams_of[3], 1), 0, 1)
    level_set = gaussian(streams_of[4], (NZ, NX, NY), 1.0, 6.0, ((1, 4), (2, 8)), jnp.float32)
    band_flag = draw_band_flag(jax.random.fold_in(streams_of[6], 71), 0)
    return dict(enthalpy=enthalpy, heat_cap=heat_cap, conductivity=conductivity, phase=phase, level_set=level_set, band_flag=band_flag)


DT_HEAT = 0.08
LATENT_HEAT = 1.5
GROWTH_RATE = 0.5
MELT_POINT = 0.25
DT_LEVEL = 0.25
WENO_FLOOR = 1e-06

def flux_of(temper, conduct):
    center = temper[:, 1:-1, 1:-1]
    kcenter = conduct[:, 1:-1, 1:-1]
    neighbours = ((temper[:, 2:, 1:-1], conduct[:, 2:, 1:-1]), (temper[:, :-2, 1:-1], conduct[:, :-2, 1:-1]), (temper[:, 1:-1, 2:], conduct[:, 1:-1, 2:]), (temper[:, 1:-1, :-2], conduct[:, 1:-1, :-2]), (jnp.concatenate([center[1:], center[-1:]], 0), jnp.concatenate([kcenter[1:], kcenter[-1:]], 0)), (jnp.concatenate([center[:1], center[:-1]], 0), jnp.concatenate([kcenter[:1], kcenter[:-1]], 0)))
    flux_sum = jnp.zeros_like(center)
    for other_temp, other_cond in neighbours:
        flux_sum = flux_sum + jnp.sqrt(kcenter * other_cond) * (other_temp - center)
    return flux_sum

def shrink(array, reach):
    return array[reach:array.shape[0] - reach, reach:array.shape[1] - reach, reach:array.shape[2] - reach]

def weno_side(first, second, third, fourth, fifth):
    cand_one = first / 3.0 - 7.0 * second / 6.0 + 11.0 * third / 6.0
    cand_two = -second / 6.0 + 5.0 * third / 6.0 + fourth / 3.0
    cand_three = third / 3.0 + 5.0 * fourth / 6.0 - fifth / 6.0
    smooth_one = 13.0 / 12.0 * (first - 2.0 * second + third) * (first - 2.0 * second + third) + 0.25 * (first - 4.0 * second + 3.0 * third) * (first - 4.0 * second + 3.0 * third)
    smooth_two = 13.0 / 12.0 * (second - 2.0 * third + fourth) * (second - 2.0 * third + fourth) + 0.25 * (second - fourth) * (second - fourth)
    smooth_three = 13.0 / 12.0 * (third - 2.0 * fourth + fifth) * (third - 2.0 * fourth + fifth) + 0.25 * (3.0 * third - 4.0 * fourth + fifth) * (3.0 * third - 4.0 * fourth + fifth)
    alpha_one = 0.1 / ((WENO_FLOOR + smooth_one) * (WENO_FLOOR + smooth_one))
    alpha_two = 0.6 / ((WENO_FLOOR + smooth_two) * (WENO_FLOOR + smooth_two))
    alpha_three = 0.3 / ((WENO_FLOOR + smooth_three) * (WENO_FLOOR + smooth_three))
    return (alpha_one * cand_one + alpha_two * cand_two + alpha_three * cand_three) / (alpha_one + alpha_two + alpha_three)

def smooth_sweep(speed, weights):
    center = shrink(speed, 1)
    accum = center
    weight_sum = jnp.ones_like(center)
    before_after = ((speed[:-2, 1:-1, 1:-1], speed[2:, 1:-1, 1:-1]), (speed[1:-1, :-2, 1:-1], speed[1:-1, 2:, 1:-1]), (speed[1:-1, 1:-1, :-2], speed[1:-1, 1:-1, 2:]))
    for direction in range(3):
        inner_weight = shrink(weights[direction], 1)
        accum = accum + inner_weight * (before_after[direction][0] + before_after[direction][1])
        weight_sum = weight_sum + 2.0 * inner_weight
    return accum / weight_sum

def update_block(level, temper):
    grad_zero = (level[2:, 1:-1, 1:-1] - level[:-2, 1:-1, 1:-1]) * 0.5
    grad_one = (level[1:-1, 2:, 1:-1] - level[1:-1, :-2, 1:-1]) * 0.5
    grad_two = (level[1:-1, 1:-1, 2:] - level[1:-1, 1:-1, :-2]) * 0.5
    norm_sq = grad_zero * grad_zero + grad_one * grad_one + grad_two * grad_two + 1.0
    weights = (grad_zero * grad_zero / norm_sq, grad_one * grad_one / norm_sq, grad_two * grad_two / norm_sq)
    speed = GROWTH_RATE * (MELT_POINT - shrink(temper, 1))
    speed = smooth_sweep(speed, weights)
    weights = tuple((shrink(weight, 1) for weight in weights))
    speed = smooth_sweep(speed, weights)
    grow_sum = jnp.zeros_like(speed)
    recede_sum = jnp.zeros_like(speed)
    for direction in range(3):
        moved = jnp.moveaxis(level, direction, 0)[:, 3:-3, 3:-3]
        diffs = moved[1:] - moved[:-1]
        length = diffs.shape[0] - 5
        parts = [diffs[offset:offset + length] for offset in range(6)]
        minus = jnp.moveaxis(weno_side(parts[0], parts[1], parts[2], parts[3], parts[4]), 0, direction)
        plus = jnp.moveaxis(weno_side(parts[5], parts[4], parts[3], parts[2], parts[1]), 0, direction)
        minus_pos = jnp.maximum(minus, 0.0)
        minus_neg = jnp.minimum(minus, 0.0)
        plus_pos = jnp.maximum(plus, 0.0)
        plus_neg = jnp.minimum(plus, 0.0)
        grow_sum = grow_sum + jnp.maximum(minus_pos * minus_pos, plus_neg * plus_neg)
        recede_sum = recede_sum + jnp.maximum(minus_neg * minus_neg, plus_pos * plus_pos)
    grad_norm = jnp.sqrt(jnp.where(speed >= 0.0, grow_sum, recede_sum) + 1e-06)
    return shrink(level, 3) - DT_LEVEL * speed * grad_norm

def wrap_pad(array, width):
    return jnp.pad(array, ((0, 0), (width, width), (width, width)), mode='wrap')

def reference(enthalpy, heat_cap, conductivity, phase, level_set, band_flag):
    liquid = phase.astype(jnp.float32)
    excess = enthalpy - LATENT_HEAT * liquid
    temp_zero = excess / heat_cap
    cond_pad = wrap_pad(conductivity, 1)
    excess_one = excess + DT_HEAT * flux_of(wrap_pad(temp_zero, 1), cond_pad)
    temp_one = excess_one / heat_cap
    excess_two = excess_one + DT_HEAT * flux_of(wrap_pad(temp_one, 1), cond_pad)
    enthalpy_out = excess_two + LATENT_HEAT * liquid
    temp_two = excess_two / heat_cap
    level_pad = jnp.pad(wrap_pad(level_set, 3), ((3, 3), (0, 0), (0, 0)), mode='edge')
    temp_pad = jnp.pad(wrap_pad(temp_two, 3), ((3, 3), (0, 0), (0, 0)), mode='edge')

    def column_update(column):
        start = column * TILE
        zero_start = jnp.zeros((), jnp.int32)
        level_col = lax.dynamic_slice(level_pad, (zero_start, start, zero_start), (NZ + 6, TILE + 6, NY + 6))
        temp_col = lax.dynamic_slice(temp_pad, (zero_start, start, zero_start), (NZ + 6, TILE + 6, NY + 6))
        return update_block(level_col, temp_col)
    updated = lax.map(column_update, jnp.arange(NX // TILE, dtype=jnp.int32))
    updated = jnp.transpose(updated, (1, 0, 2, 3)).reshape(NZ, NX, NY)
    cell_mask = jnp.repeat(jnp.repeat(jnp.repeat(band_flag, TILE, 0), TILE, 1), TILE, 2) == 1
    level_out = jnp.where(cell_mask, updated, level_set)
    return (enthalpy_out, level_out)
```

```python
import functools

import jax
import jax.numpy as jnp
from jax import lax
from jax.experimental import pallas as pl
from jax.experimental.pallas import tpu as pltpu
from jax.sharding import PartitionSpec as P

TILE = 32
DT_HEAT = 0.08
LATENT_HEAT = 1.5
GROWTH_RATE = 0.5
MELT_POINT = 0.25
DT_LEVEL = 0.25
WENO_FLOOR = 1e-06

OFF = 16
LO, HI = 0, 1
F32 = jnp.float32


def recip(value):
    guess = pl.reciprocal(value, approx=True)
    return guess * (2.0 - value * guess)


def weno(d0, d1, d2, d3, d4, d5):
    c0, c1, c2, c3, c4 = d1 - d0, d2 - d1, d3 - d2, d4 - d3, d5 - d4
    e1, e2, e3, e4 = c1 - c0, c2 - c1, c3 - c2, c4 - c3
    f1, f2, f3, f4 = [(13.0 / 3.0) * e * e + 4.0 * WENO_FLOOR for e in (e1, e2, e3, e4)]
    two1, two2, two3 = c1 + c1, c2 + c2, c3 + c3
    tri1, tri2, tri3 = two1 + c1, two2 + c2, two3 + c3

    def side(base, qa, qb, qc, na, nb, nc):
        ab, ac, bc = qa * qb, qa * qc, qb * qc
        wa, wb, wc = bc * bc, 6.0 * (ac * ac), 3.0 * (ab * ab)
        return base + (wa * na + wb * nb + wc * nc) * recip(6.0 * (wa + wb + wc))

    def sq(v):
        return v * v

    minus = side(
        d2, f1 + sq(two1 + e1), f2 + sq(c1 + c2), f3 + sq(two2 - e3),
        tri1 + (e1 + e1), c1 + two2, tri2 - e3,
    )
    plus_neg = side(
        -d3, f4 + sq(e4 - two3), f3 + sq(c2 + c3), f2 + sq(two2 + e2),
        tri3 - (e4 + e4), c3 + two2, tri2 + e2,
    )
    grow = jnp.maximum(jnp.maximum(minus, plus_neg), 0.0)
    fall = jnp.minimum(jnp.minimum(minus, plus_neg), 0.0)
    return grow * grow, fall * fall


def kernel(
    ngx, ngy, chunk,
    flag, enth, heat, cond, phase, level, eout, lout,
    lv, hl, sq, ua, ub, ihc, tm, ex, wsum, s0, hs0, s1, hs1, cx, ch, gs, rs,
    sx1, rx1, sy1, ry1, sxl, rxl, syl, ryl, sx2, rx2, sy2, ry2, sx3, rx3, sy3, ry3,
    send_sem, recv_sem,
):
    nz, nx, ny = enth.shape
    top = OFF + nx
    gx, gy = lax.axis_index("gx"), lax.axis_index("gy")
    west, east = lax.rem(gx + ngx - 1, ngx), lax.rem(gx + 1, ngx)
    south, north = lax.rem(gy + ngy - 1, ngy), lax.rem(gy + 1, ngy)
    others = [(a, b) for a in (west, gx, east) for b in (south, gy, north) if not (a is gx and b is gy)]
    barrier = pltpu.get_barrier_semaphore()
    for other in others:
        pl.semaphore_signal(barrier, inc=1, device_id=other, device_id_type=pl.DeviceIdType.MESH)

    lane = lax.broadcasted_iota(jnp.int32, (1, ny), 1)
    own = slice(OFF, top)
    count = [0]

    def copy(src, dst, where):
        i = count[0]
        count[0] += 1
        c = pltpu.make_async_remote_copy(
            src_ref=src, dst_ref=dst, send_sem=send_sem.at[i], recv_sem=recv_sem.at[i],
            device_id=where, device_id_type=pl.DeviceIdType.MESH,
        )
        c.start()
        return c

    def send_x(sx, rx):
        return [
            copy(sx.at[LO], rx.at[HI], (west, gy)),
            copy(sx.at[HI], rx.at[LO], (east, gy)),
        ]

    def send_y(sy, ry):
        return [copy(sy, ry.at[HI], (gx, south)), copy(sy, ry.at[LO], (gx, north))]

    def send_y_corners(sy, ry):
        out = []
        for side, where in ((HI, south), (LO, north)):
            r = ry.at[side]
            out.append(copy(sy, r.at[:, 8 : 8 + nx], (gx, where)))
            out.append(copy(sy.at[:, 0:8], r.at[:, 8 + nx : 16 + nx], (west, where)))
            out.append(copy(sy.at[:, nx - 8 : nx], r.at[:, 0:8], (east, where)))
        return out

    def up(x, h, k=1):
        return pltpu.roll(jnp.where(lane < k, h, x), ny - k, 1)

    def down(x, h, k=1):
        return pltpu.roll(jnp.where(lane >= ny - k, h, x), k, 1)

    def pack(x, z, width, acc):
        group = ny // (2 * width)
        g = lax.rem(z, group)
        return jnp.where(lane // (2 * width) == g, pltpu.roll(x, g * (2 * width) + width, 1), acc)

    def unpack(packed, z, width):
        group = ny // (2 * width)
        g = lax.rem(z, group)
        return pltpu.roll(packed, ny - (g * (2 * width) + width), 1)

    def merged(from_lo, from_hi, width):
        return jnp.where(lane % (2 * width) >= width, from_hi, from_lo)

    def rows_of(ref, row):
        rows = ref.shape[1]
        return ref.reshape(ref.shape[0] * rows, ny), rows, row

    def get_row(ref, row, z0=0):
        flat, rows, row = rows_of(ref, row)
        return flat[pl.ds(z0 * rows + row, nz, stride=rows), :]

    def put_row(ref, row, value, z0=0):
        flat, rows, row = rows_of(ref, row)
        flat[pl.ds(z0 * rows + row, nz, stride=rows), :] = value

    def start(z, acc):
        accu, accs = acc
        e = enth[z] - LATENT_HEAT * phase[z].astype(F32)
        r = 1.0 / heat[z]
        t = e * r
        s = jnp.sqrt(cond[z])
        u = s * t
        ihc[z], tm[z], ex[z] = r, t, e
        sq[z, own], ua[z, own] = s, u
        return pack(u, z, 1, accu), pack(s, z, 1, accs)

    zero = jnp.zeros((nx, ny), F32)
    sy1[0], sy1[1] = lax.fori_loop(0, nz, start, (zero, zero))
    for i, ref in enumerate((ua, sq)):
        sx1[LO, i] = get_row(ref, OFF)
        sx1[HI, i] = get_row(ref, top - 1)
    pl.semaphore_wait(barrier, len(others))
    first = send_x(sx1, rx1) + send_y(sy1, ry1)

    def level_group(q, _):
        def one(g, acc):
            z = q * 16 + g
            x = level[z]
            lv[z + 3, own] = x
            return pack(x, z, 4, acc)

        syl[q] = lax.fori_loop(0, 16, one, zero)
        return 0

    lax.fori_loop(0, nz // 16, level_group, 0)
    for k in range(3):
        sxl[LO, k] = get_row(lv, OFF + k, 3)
        sxl[HI, k] = get_row(lv, top - 3 + k, 3)
    levels = send_x(sxl, rxl) + send_y_corners(syl, ryl)

    def ends(ref, rows):
        for k in range(3):
            ref[k, rows] = ref[3, rows]
            ref[nz + 3 + k, rows] = ref[nz + 2, rows]

    ends(lv, own)

    def weno_z(z, _):
        for r in range(0, nx, chunk):
            at = slice(OFF + r, OFF + r + chunk)
            v = [lv[z + k, at] for k in range(7)]
            g, f = weno(*[v[k + 1] - v[k] for k in range(6)])
            gs[z, r : r + chunk], rs[z, r : r + chunk] = g, f
        return 0

    lax.fori_loop(0, nz, weno_z, 0)

    def around(ref, z, packed):
        x = ref[z, own]
        h = unpack(packed, z, 1)
        return (
            ref[jnp.maximum(z - 1, 0), own] + ref[jnp.minimum(z + 1, nz - 1), own]
            + (ref[z, OFF - 1 : top - 1] + ref[z, OFF + 1 : top + 1])
            + (up(x, h) + down(x, h))
        )

    for c in first:
        c.wait()
    for i, ref in enumerate((ua, sq)):
        put_row(ref, OFF - 1, rx1[LO, i])
        put_row(ref, top, rx1[HI, i])

    def substep1(z, acc):
        pu = merged(ry1[LO, 0], ry1[HI, 0], 1)
        ps = merged(ry1[LO, 1], ry1[HI, 1], 1)
        w = around(sq, z, ps)
        s = sq[z, own]
        e = ex[z] + DT_HEAT * (s * (around(ua, z, pu) - tm[z] * w))
        t = e * ihc[z]
        u = s * t
        wsum[z], ex[z], tm[z], ub[z, own] = w, e, t, u
        return pack(u, z, 1, acc)

    sy2[...] = lax.fori_loop(0, nz, substep1, zero)
    sx2[LO] = get_row(ub, OFF)
    sx2[HI] = get_row(ub, top - 1)
    second = send_x(sx2, rx2) + send_y(sy2, ry2)

    for c in levels:
        c.wait()
    for k in range(3):
        put_row(lv, OFF - 3 + k, rxl[LO, k], 3)
        put_row(lv, top + k, rxl[HI, k], 3)
    wide = slice(OFF - 8, top + 8)

    def level_halo(z, _):
        q = z // 16
        hl[z + 3, wide] = unpack(merged(ryl[LO, q], ryl[HI, q], 4), z, 4)
        return 0

    lax.fori_loop(0, nz, level_halo, 0)
    ends(lv, wide)
    ends(hl, wide)

    def weno_xy(z, _):
        half = z // TILE
        masks = [jnp.where(flag[half, 0, j] == 1, -DT_LEVEL, 0.0) for j in range(ny // TILE)]
        mask = jnp.full((1, ny), masks[0])
        for j in range(1, ny // TILE):
            mask = jnp.where(lane >= j * TILE, masks[j], mask)
        for r in range(0, nx, chunk):
            a = OFF + r
            x = lv[z + 3, a : a + chunk]
            v = [x if k == 3 else lv[z + 3, a + k - 3 : a + k - 3 + chunk] for k in range(7)]
            g1, f1 = weno(*[v[k + 1] - v[k] for k in range(6)])
            h = hl[z + 3, a : a + chunk]
            v = [down(x, h, k) for k in (3, 2, 1)] + [x] + [up(x, h, k) for k in (1, 2, 3)]
            g2, f2 = weno(*[v[k + 1] - v[k] for k in range(6)])
            at = slice(r, r + chunk)
            gs[z, at] = mask * jnp.sqrt(gs[z, at] + g1 + g2 + 1e-06)
            rs[z, at] = mask * jnp.sqrt(rs[z, at] + f1 + f2 + 1e-06)
        return 0

    def coefs(out, oz, orow, main, side, z, a, rows):
        at = slice(a, a + rows)
        x, h = main[z + 3, at], side[z + 3, at]
        d0 = main[z + 4, at] - main[z + 2, at]
        d1 = main[z + 3, a + 1 : a + 1 + rows] - main[z + 3, a - 1 : a - 1 + rows]
        d2 = up(x, h) - down(x, h)
        d0, d1, d2 = d0 * d0, d1 * d1, d2 * d2
        total = d0 + d1 + d2
        inv = recip(4.0 + 3.0 * total)
        to = slice(orow, orow + rows)
        out[0, oz, to] = (4.0 + total) * inv
        out[1, oz, to] = d0 * inv
        out[2, oz, to] = d1 * inv
        out[3, oz, to] = d2 * inv

    def coefs_x(i, _):
        coefs(cx, i, 0, lv, hl, i - 1, OFF - 8, nx + 16)
        return 0

    def coefs_h(z, _):
        coefs(ch, z, 0, hl, lv, z, OFF, nx)
        return 0

    lax.fori_loop(0, nz // 2, weno_xy, 0)

    for c in second:
        c.wait()
    put_row(ub, OFF - 1, rx2[LO])
    put_row(ub, top, rx2[HI])

    def substep2_group(q, _):
        def substep2(g, acc):
            z = q * 32 + g
            pu = merged(ry2[LO], ry2[HI], 1)
            e = ex[z] + DT_HEAT * (sq[z, own] * (around(ub, z, pu) - tm[z] * wsum[z]))
            eout[z] = e + LATENT_HEAT * phase[z].astype(F32)
            s = GROWTH_RATE * (MELT_POINT - e * ihc[z])
            s0[z, own] = s
            return pack(s, z, 2, acc)

        sy3[q] = lax.fori_loop(0, 32, substep2, zero)
        return 0

    lax.fori_loop(0, nz // 32, substep2_group, 0)
    for k in range(2):
        sx3[LO, k] = get_row(s0, OFF + k)
        sx3[HI, k] = get_row(s0, top - 2 + k)
    third = send_x(sx3, rx3) + send_y_corners(sy3, ry3)

    lax.fori_loop(nz // 2, nz, weno_xy, 0)
    lax.fori_loop(0, nz + 2, coefs_x, 0)
    lax.fori_loop(0, nz, coefs_h, 0)

    for c in third:
        c.wait()
    for k in range(2):
        put_row(s0, OFF - 2 + k, rx3[LO, k])
        put_row(s0, top + k, rx3[HI, k])

    def speed_halo(z, _):
        q = z // 32
        hs0[z, wide] = unpack(merged(ry3[LO, q], ry3[HI, q], 2), z, 2)
        return 0

    lax.fori_loop(0, nz, speed_halo, 0)

    def clamp(z):
        return jnp.minimum(jnp.maximum(z, 0), nz - 1)

    def sweep(c, cz, crow, main, zb, zc, za, side, a, rows):
        at, to = slice(a, a + rows), slice(crow, crow + rows)
        x = main[zc, at]
        return (
            c[0, cz, to] * x
            + c[1, cz, to] * (main[zb, at] + main[za, at])
            + c[2, cz, to] * (main[zc, a - 1 : a - 1 + rows] + main[zc, a + 1 : a + 1 + rows])
            + c[3, cz, to] * (up(x, side) + down(x, side))
        )

    def sweep1_x(i, _):
        b, m, t = clamp(i - 2), clamp(i - 1), clamp(i)
        s1[i, wide] = sweep(cx, i, 0, s0, b, m, t, hs0[m, wide], OFF - 8, nx + 16)
        return 0

    lax.fori_loop(0, nz + 2, sweep1_x, 0)

    def sweep1_h(z, _):
        hs1[z] = sweep(ch, z, 0, hs0, clamp(z - 1), z, clamp(z + 1), s0[z, own], OFF, nx)
        return 0

    lax.fori_loop(0, nz, sweep1_h, 0)

    def last(z, _):
        s = sweep(cx, z + 1, 8, s1, z, z + 1, z + 2, hs1[z], OFF, nx)
        lout[z] = level[z] + s * jnp.where(s >= 0.0, gs[z], rs[z])
        return 0

    lax.fori_loop(0, nz, last, 0)


CHUNK = 16


def body(ngx, ngy, enthalpy, heat_cap, conductivity, phase, level_set, band_flag):
    nz, nx, ny = enthalpy.shape
    tall = nx + 2 * OFF

    def vmem(*shape):
        return pltpu.VMEM(shape, F32)

    copies = 4 + 8 + 4 + 8
    scratch = [
        vmem(nz + 6, tall, ny),
        vmem(nz + 6, tall, ny),
        vmem(nz, tall, ny),
        vmem(nz, tall, ny),
        vmem(nz, tall, ny),
        vmem(nz, nx, ny),
        vmem(nz, nx, ny),
        vmem(nz, nx, ny),
        vmem(nz, nx, ny),
        vmem(nz, tall, ny),
        vmem(nz, tall, ny),
        vmem(nz + 2, tall, ny),
        vmem(nz, nx, ny),
        vmem(4, nz + 2, nx + 16, ny),
        vmem(4, nz, nx, ny),
        vmem(nz, nx, ny),
        vmem(nz, nx, ny),
        vmem(2, 2, nz, ny), vmem(2, 2, nz, ny), vmem(2, nx, ny), vmem(2, 2, nx, ny),
        vmem(2, 3, nz, ny), vmem(2, 3, nz, ny), vmem(nz // 16, nx, ny), vmem(2, nz // 16, nx + 16, ny),
        vmem(2, nz, ny), vmem(2, nz, ny), vmem(nx, ny), vmem(2, nx, ny),
        vmem(2, 2, nz, ny), vmem(2, 2, nz, ny), vmem(nz // 32, nx, ny), vmem(2, nz // 32, nx + 16, ny),
        pltpu.SemaphoreType.DMA((copies,)),
        pltpu.SemaphoreType.DMA((copies,)),
    ]
    whole = pl.BlockSpec(memory_space=pltpu.VMEM)
    out = jax.ShapeDtypeStruct((nz, nx, ny), F32)
    return pl.pallas_call(
        functools.partial(kernel, ngx, ngy, CHUNK),
        out_shape=(out, out),
        in_specs=[pl.BlockSpec(memory_space=pltpu.SMEM)] + [whole] * 5,
        out_specs=(whole, whole),
        scratch_shapes=scratch,
        compiler_params=pltpu.CompilerParams(
            collective_id=0, has_side_effects=True, vmem_limit_bytes=60 * 1024 * 1024
        ),
    )(band_flag, enthalpy, heat_cap, conductivity, phase, level_set)


def solution(mesh):
    spec = P(None, "gx", "gy")
    return jax.shard_map(
        functools.partial(body, mesh.shape["gx"], mesh.shape["gy"]),
        mesh=mesh, in_specs=(spec,) * 6, out_specs=(spec, spec), check_vma=False,
    )
```

```python
import functools

import jax
import jax.numpy as jnp
from jax import lax
from jax.experimental import pallas as pl
from jax.experimental.pallas import tpu as pltpu
from jax.sharding import PartitionSpec as P

TILE = 32
DT_HEAT = 0.08
LATENT_HEAT = 1.5
GROWTH_RATE = 0.5
MELT_POINT = 0.25
DT_LEVEL = 0.25
WENO_FLOOR = 1e-06

OFF = 16
LO, HI = 0, 1
U_START, U_SUB, U_COEF, U_SWEEP, U_LAST, U_WENO = 8, 8, 8, 8, 8, 2
F32 = jnp.float32


def recip(value):
    guess = pl.reciprocal(value, approx=True)
    return guess * (2.0 - value * guess)


def loop(low, high, step, init, unroll):
    whole = (high - low) // unroll

    def several(i, value):
        for j in range(unroll):
            value = step(low + i * unroll + j, value)
        return value

    value = lax.fori_loop(0, whole, several, init)
    for i in range(low + whole * unroll, high):
        value = step(i, value)
    return value


def weno(d0, d1, d2, d3, d4, d5):
    c0, c1, c2, c3, c4 = d1 - d0, d2 - d1, d3 - d2, d4 - d3, d5 - d4
    e1, e2, e3, e4 = c1 - c0, c2 - c1, c3 - c2, c4 - c3
    f1, f2, f3, f4 = [(13.0 / 3.0) * e * e + 4.0 * WENO_FLOOR for e in (e1, e2, e3, e4)]
    two1, two2, two3 = c1 + c1, c2 + c2, c3 + c3
    tri1, tri2, tri3 = two1 + c1, two2 + c2, two3 + c3

    def side(base, qa, qb, qc, na, nb, nc):
        ab, ac, bc = qa * qb, qa * qc, qb * qc
        wa, wb, wc = bc * bc, 6.0 * (ac * ac), 3.0 * (ab * ab)
        return base + (wa * na + wb * nb + wc * nc) * recip(6.0 * (wa + wb + wc))

    def sq(v):
        return v * v

    minus = side(
        d2, f1 + sq(two1 + e1), f2 + sq(c1 + c2), f3 + sq(two2 - e3),
        tri1 + (e1 + e1), c1 + two2, tri2 - e3,
    )
    plus_neg = side(
        -d3, f4 + sq(e4 - two3), f3 + sq(c2 + c3), f2 + sq(two2 + e2),
        tri3 - (e4 + e4), c3 + two2, tri2 + e2,
    )
    grow = jnp.maximum(jnp.maximum(minus, plus_neg), 0.0)
    fall = jnp.minimum(jnp.minimum(minus, plus_neg), 0.0)
    return grow * grow, fall * fall


def kernel(
    ngx, ngy, chunk,
    flag, enth, heat, cond, phase, level, eout, lout,
    lv, hl, sq, ua, ub, ihc, tm, ex, wsum, s0, hs0, s1, hs1, cx, ch, gs, rs,
    sx1, rx1, sy1, ry1, sxl, rxl, syl, ryl, sx2, rx2, sy2, ry2, sx3, rx3, sy3, ry3,
    send_sem, recv_sem,
):
    nz, nx, ny = enth.shape
    top = OFF + nx
    gx, gy = lax.axis_index("gx"), lax.axis_index("gy")
    west, east = lax.rem(gx + ngx - 1, ngx), lax.rem(gx + 1, ngx)
    south, north = lax.rem(gy + ngy - 1, ngy), lax.rem(gy + 1, ngy)
    others = [(a, b) for a in (west, gx, east) for b in (south, gy, north) if not (a is gx and b is gy)]
    barrier = pltpu.get_barrier_semaphore()
    for other in others:
        pl.semaphore_signal(barrier, inc=1, device_id=other, device_id_type=pl.DeviceIdType.MESH)

    lane = lax.broadcasted_iota(jnp.int32, (1, ny), 1)
    own = slice(OFF, top)
    count = [0]

    def copy(src, dst, where):
        i = count[0]
        count[0] += 1
        c = pltpu.make_async_remote_copy(
            src_ref=src, dst_ref=dst, send_sem=send_sem.at[i], recv_sem=recv_sem.at[i],
            device_id=where, device_id_type=pl.DeviceIdType.MESH,
        )
        c.start()
        return c

    def send_x(sx, rx):
        return [
            copy(sx.at[LO], rx.at[HI], (west, gy)),
            copy(sx.at[HI], rx.at[LO], (east, gy)),
        ]

    def send_y(sy, ry):
        return [copy(sy, ry.at[HI], (gx, south)), copy(sy, ry.at[LO], (gx, north))]

    def send_y_corners(sy, ry):
        out = []
        for side, where in ((HI, south), (LO, north)):
            r = ry.at[side]
            out.append(copy(sy, r.at[:, 8 : 8 + nx], (gx, where)))
            out.append(copy(sy.at[:, 0:8], r.at[:, 8 + nx : 16 + nx], (west, where)))
            out.append(copy(sy.at[:, nx - 8 : nx], r.at[:, 0:8], (east, where)))
        return out

    def up(x, h, k=1):
        return pltpu.roll(jnp.where(lane < k, h, x), ny - k, 1)

    def down(x, h, k=1):
        return pltpu.roll(jnp.where(lane >= ny - k, h, x), k, 1)

    def pack(x, z, width, acc):
        group = ny // (2 * width)
        g = lax.rem(z, group)
        return jnp.where(lane // (2 * width) == g, pltpu.roll(x, g * (2 * width) + width, 1), acc)

    def unpack(packed, z, width):
        group = ny // (2 * width)
        g = lax.rem(z, group)
        return pltpu.roll(packed, ny - (g * (2 * width) + width), 1)

    def merged(from_lo, from_hi, width):
        return jnp.where(lane % (2 * width) >= width, from_hi, from_lo)

    def rows_of(ref, row):
        rows = ref.shape[1]
        return ref.reshape(ref.shape[0] * rows, ny), rows, row

    def get_row(ref, row, z0=0):
        flat, rows, row = rows_of(ref, row)
        return flat[pl.ds(z0 * rows + row, nz, stride=rows), :]

    def put_row(ref, row, value, z0=0):
        flat, rows, row = rows_of(ref, row)
        flat[pl.ds(z0 * rows + row, nz, stride=rows), :] = value

    def start(z, acc):
        accu, accs = acc
        e = enth[z] - LATENT_HEAT * phase[z].astype(F32)
        r = 1.0 / heat[z]
        t = e * r
        s = jnp.sqrt(cond[z])
        u = s * t
        ihc[z], tm[z], ex[z] = r, t, e
        sq[z, own], ua[z, own] = s, u
        return pack(u, z, 1, accu), pack(s, z, 1, accs)

    zero = jnp.zeros((nx, ny), F32)
    sy1[0], sy1[1] = loop(0, nz, start, (zero, zero), U_START)
    for i, ref in enumerate((ua, sq)):
        sx1[LO, i] = get_row(ref, OFF)
        sx1[HI, i] = get_row(ref, top - 1)
    pl.semaphore_wait(barrier, len(others))
    first = send_x(sx1, rx1) + send_y(sy1, ry1)

    def level_group(q, _):
        def one(g, acc):
            z = q * 16 + g
            x = level[z]
            lv[z + 3, own] = x
            return pack(x, z, 4, acc)

        syl[q] = loop(0, 16, one, zero, 16)
        return 0

    lax.fori_loop(0, nz // 16, level_group, 0)
    for k in range(3):
        sxl[LO, k] = get_row(lv, OFF + k, 3)
        sxl[HI, k] = get_row(lv, top - 3 + k, 3)
    levels = send_x(sxl, rxl) + send_y_corners(syl, ryl)

    def ends(ref, rows):
        for k in range(3):
            ref[k, rows] = ref[3, rows]
            ref[nz + 3 + k, rows] = ref[nz + 2, rows]

    ends(lv, own)

    def weno_z(z, _):
        for r in range(0, nx, chunk):
            at = slice(OFF + r, OFF + r + chunk)
            v = [lv[z + k, at] for k in range(7)]
            g, f = weno(*[v[k + 1] - v[k] for k in range(6)])
            gs[z, r : r + chunk], rs[z, r : r + chunk] = g, f
        return 0

    loop(0, nz, weno_z, 0, U_WENO)

    def around(ref, z, packed):
        x = ref[z, own]
        h = unpack(packed, z, 1)
        return (
            ref[jnp.maximum(z - 1, 0), own] + ref[jnp.minimum(z + 1, nz - 1), own]
            + (ref[z, OFF - 1 : top - 1] + ref[z, OFF + 1 : top + 1])
            + (up(x, h) + down(x, h))
        )

    for c in first:
        c.wait()
    for i, ref in enumerate((ua, sq)):
        put_row(ref, OFF - 1, rx1[LO, i])
        put_row(ref, top, rx1[HI, i])

    def substep1(z, acc):
        pu = merged(ry1[LO, 0], ry1[HI, 0], 1)
        ps = merged(ry1[LO, 1], ry1[HI, 1], 1)
        w = around(sq, z, ps)
        s = sq[z, own]
        e = ex[z] + DT_HEAT * (s * (around(ua, z, pu) - tm[z] * w))
        t = e * ihc[z]
        u = s * t
        wsum[z], ex[z], tm[z], ub[z, own] = w, e, t, u
        return pack(u, z, 1, acc)

    sy2[...] = loop(0, nz, substep1, zero, U_SUB)
    sx2[LO] = get_row(ub, OFF)
    sx2[HI] = get_row(ub, top - 1)
    second = send_x(sx2, rx2) + send_y(sy2, ry2)

    for c in levels:
        c.wait()
    for k in range(3):
        put_row(lv, OFF - 3 + k, rxl[LO, k], 3)
        put_row(lv, top + k, rxl[HI, k], 3)
    wide = slice(OFF - 8, top + 8)

    def level_halo(z, _):
        q = z // 16
        hl[z + 3, wide] = unpack(merged(ryl[LO, q], ryl[HI, q], 4), z, 4)
        return 0

    loop(0, nz, level_halo, 0, 8)
    ends(lv, wide)
    ends(hl, wide)

    def weno_xy(z, _):
        half = z // TILE
        masks = [jnp.where(flag[half, 0, j] == 1, -DT_LEVEL, 0.0) for j in range(ny // TILE)]
        mask = jnp.full((1, ny), masks[0])
        for j in range(1, ny // TILE):
            mask = jnp.where(lane >= j * TILE, masks[j], mask)
        for r in range(0, nx, chunk):
            a = OFF + r
            x = lv[z + 3, a : a + chunk]
            v = [x if k == 3 else lv[z + 3, a + k - 3 : a + k - 3 + chunk] for k in range(7)]
            g1, f1 = weno(*[v[k + 1] - v[k] for k in range(6)])
            h = hl[z + 3, a : a + chunk]
            v = [down(x, h, k) for k in (3, 2, 1)] + [x] + [up(x, h, k) for k in (1, 2, 3)]
            g2, f2 = weno(*[v[k + 1] - v[k] for k in range(6)])
            at = slice(r, r + chunk)
            gs[z, at] = mask * jnp.sqrt(gs[z, at] + g1 + g2 + 1e-06)
            rs[z, at] = mask * jnp.sqrt(rs[z, at] + f1 + f2 + 1e-06)
        return 0

    def coefs(out, oz, orow, main, side, z, a, rows):
        at = slice(a, a + rows)
        x, h = main[z + 3, at], side[z + 3, at]
        d0 = main[z + 4, at] - main[z + 2, at]
        d1 = main[z + 3, a + 1 : a + 1 + rows] - main[z + 3, a - 1 : a - 1 + rows]
        d2 = up(x, h) - down(x, h)
        d0, d1, d2 = d0 * d0, d1 * d1, d2 * d2
        total = d0 + d1 + d2
        inv = recip(4.0 + 3.0 * total)
        to = slice(orow, orow + rows)
        out[0, oz, to] = (4.0 + total) * inv
        out[1, oz, to] = d0 * inv
        out[2, oz, to] = d1 * inv
        out[3, oz, to] = d2 * inv

    def coefs_x(i, _):
        coefs(cx, i, 0, lv, hl, i - 1, OFF - 8, nx + 16)
        return 0

    def coefs_h(z, _):
        coefs(ch, z, 0, hl, lv, z, OFF, nx)
        return 0

    loop(0, nz // 2, weno_xy, 0, U_WENO)

    for c in second:
        c.wait()
    put_row(ub, OFF - 1, rx2[LO])
    put_row(ub, top, rx2[HI])

    def substep2_group(q, _):
        def substep2(g, acc):
            z = q * 32 + g
            pu = merged(ry2[LO], ry2[HI], 1)
            e = ex[z] + DT_HEAT * (sq[z, own] * (around(ub, z, pu) - tm[z] * wsum[z]))
            eout[z] = e + LATENT_HEAT * phase[z].astype(F32)
            s = GROWTH_RATE * (MELT_POINT - e * ihc[z])
            s0[z, own] = s
            return pack(s, z, 2, acc)

        sy3[q] = loop(0, 32, substep2, zero, U_SUB)
        return 0

    lax.fori_loop(0, nz // 32, substep2_group, 0)
    for k in range(2):
        sx3[LO, k] = get_row(s0, OFF + k)
        sx3[HI, k] = get_row(s0, top - 2 + k)
    third = send_x(sx3, rx3) + send_y_corners(sy3, ry3)

    loop(nz // 2, nz, weno_xy, 0, U_WENO)
    loop(0, nz + 2, coefs_x, 0, U_COEF)
    loop(0, nz, coefs_h, 0, U_COEF)

    for c in third:
        c.wait()
    for k in range(2):
        put_row(s0, OFF - 2 + k, rx3[LO, k])
        put_row(s0, top + k, rx3[HI, k])

    def speed_halo(z, _):
        q = z // 32
        hs0[z, wide] = unpack(merged(ry3[LO, q], ry3[HI, q], 2), z, 2)
        return 0

    loop(0, nz, speed_halo, 0, 8)

    def clamp(z):
        return jnp.minimum(jnp.maximum(z, 0), nz - 1)

    def sweep(c, cz, crow, main, zb, zc, za, side, a, rows):
        at, to = slice(a, a + rows), slice(crow, crow + rows)
        x = main[zc, at]
        return (
            c[0, cz, to] * x
            + c[1, cz, to] * (main[zb, at] + main[za, at])
            + c[2, cz, to] * (main[zc, a - 1 : a - 1 + rows] + main[zc, a + 1 : a + 1 + rows])
            + c[3, cz, to] * (up(x, side) + down(x, side))
        )

    def sweep1_x(i, _):
        b, m, t = clamp(i - 2), clamp(i - 1), clamp(i)
        s1[i, wide] = sweep(cx, i, 0, s0, b, m, t, hs0[m, wide], OFF - 8, nx + 16)
        return 0

    loop(0, nz + 2, sweep1_x, 0, U_SWEEP)

    def sweep1_h(z, _):
        hs1[z] = sweep(ch, z, 0, hs0, clamp(z - 1), z, clamp(z + 1), s0[z, own], OFF, nx)
        return 0

    loop(0, nz, sweep1_h, 0, U_SWEEP)

    def last(z, _):
        s = sweep(cx, z + 1, 8, s1, z, z + 1, z + 2, hs1[z], OFF, nx)
        lout[z] = level[z] + s * jnp.where(s >= 0.0, gs[z], rs[z])
        return 0

    loop(0, nz, last, 0, U_LAST)


CHUNK = 16


def body(ngx, ngy, enthalpy, heat_cap, conductivity, phase, level_set, band_flag):
    nz, nx, ny = enthalpy.shape
    tall = nx + 2 * OFF

    def vmem(*shape):
        return pltpu.VMEM(shape, F32)

    copies = 4 + 8 + 4 + 8
    scratch = [
        vmem(nz + 6, tall, ny),
        vmem(nz + 6, tall, ny),
        vmem(nz, tall, ny),
        vmem(nz, tall, ny),
        vmem(nz, tall, ny),
        vmem(nz, nx, ny),
        vmem(nz, nx, ny),
        vmem(nz, nx, ny),
        vmem(nz, nx, ny),
        vmem(nz, tall, ny),
        vmem(nz, tall, ny),
        vmem(nz + 2, tall, ny),
        vmem(nz, nx, ny),
        vmem(4, nz + 2, nx + 16, ny),
        vmem(4, nz, nx, ny),
        vmem(nz, nx, ny),
        vmem(nz, nx, ny),
        vmem(2, 2, nz, ny), vmem(2, 2, nz, ny), vmem(2, nx, ny), vmem(2, 2, nx, ny),
        vmem(2, 3, nz, ny), vmem(2, 3, nz, ny), vmem(nz // 16, nx, ny), vmem(2, nz // 16, nx + 16, ny),
        vmem(2, nz, ny), vmem(2, nz, ny), vmem(nx, ny), vmem(2, nx, ny),
        vmem(2, 2, nz, ny), vmem(2, 2, nz, ny), vmem(nz // 32, nx, ny), vmem(2, nz // 32, nx + 16, ny),
        pltpu.SemaphoreType.DMA((copies,)),
        pltpu.SemaphoreType.DMA((copies,)),
    ]
    whole = pl.BlockSpec(memory_space=pltpu.VMEM)
    out = jax.ShapeDtypeStruct((nz, nx, ny), F32)
    return pl.pallas_call(
        functools.partial(kernel, ngx, ngy, CHUNK),
        out_shape=(out, out),
        in_specs=[pl.BlockSpec(memory_space=pltpu.SMEM)] + [whole] * 5,
        out_specs=(whole, whole),
        scratch_shapes=scratch,
        compiler_params=pltpu.CompilerParams(
            collective_id=0, has_side_effects=True, vmem_limit_bytes=60 * 1024 * 1024
        ),
    )(band_flag, enthalpy, heat_cap, conductivity, phase, level_set)


def solution(mesh):
    spec = P(None, "gx", "gy")
    return jax.shard_map(
        functools.partial(body, mesh.shape["gx"], mesh.shape["gy"]),
        mesh=mesh, in_specs=(spec,) * 6, out_specs=(spec, spec), check_vma=False,
    )
```

```python
import functools

import jax
import jax.numpy as jnp
from jax import lax
from jax.experimental import pallas as pl
from jax.experimental.pallas import tpu as pltpu
from jax.sharding import PartitionSpec as P

TILE = 32
DT_HEAT = 0.08
LATENT_HEAT = 1.5
GROWTH_RATE = 0.5
MELT_POINT = 0.25
DT_LEVEL = 0.25
WENO_FLOOR = 1e-06

OFF = 16
LO, HI = 0, 1
U_START, U_SUB, U_COEF, U_SWEEP, U_LAST, U_WENO = 8, 8, 8, 8, 8, 4
F32 = jnp.float32


def recip(value):
    guess = pl.reciprocal(value, approx=True)
    return guess * (2.0 - value * guess)


def loop(low, high, step, init, unroll):
    whole = (high - low) // unroll

    def several(i, value):
        for j in range(unroll):
            value = step(low + i * unroll + j, value)
        return value

    value = lax.fori_loop(0, whole, several, init)
    for i in range(low + whole * unroll, high):
        value = step(i, value)
    return value


def weno(d0, d1, d2, d3, d4, d5):
    c0, c1, c2, c3, c4 = d1 - d0, d2 - d1, d3 - d2, d4 - d3, d5 - d4
    e1, e2, e3, e4 = c1 - c0, c2 - c1, c3 - c2, c4 - c3
    f1, f2, f3, f4 = [(13.0 / 3.0) * e * e + 4.0 * WENO_FLOOR for e in (e1, e2, e3, e4)]
    two1, two2, two3 = c1 + c1, c2 + c2, c3 + c3
    tri1, tri2, tri3 = two1 + c1, two2 + c2, two3 + c3

    def side(base, qa, qb, qc, na, nb, nc):
        ab, ac, bc = qa * qb, qa * qc, qb * qc
        wa, wb, wc = bc * bc, 6.0 * (ac * ac), 3.0 * (ab * ab)
        return base + (wa * na + wb * nb + wc * nc) * recip(6.0 * (wa + wb + wc))

    def sq(v):
        return v * v

    minus = side(
        d2, f1 + sq(two1 + e1), f2 + sq(c1 + c2), f3 + sq(two2 - e3),
        tri1 + (e1 + e1), c1 + two2, tri2 - e3,
    )
    plus_neg = side(
        -d3, f4 + sq(e4 - two3), f3 + sq(c2 + c3), f2 + sq(two2 + e2),
        tri3 - (e4 + e4), c3 + two2, tri2 + e2,
    )
    grow = jnp.maximum(jnp.maximum(minus, plus_neg), 0.0)
    fall = jnp.minimum(jnp.minimum(minus, plus_neg), 0.0)
    return grow * grow, fall * fall


def kernel(
    ngx, ngy, chunk,
    flag, enth, heat, cond, phase, level, eout, lout,
    lv, hl, sq, ua, ub, ihc, tm, ex, wsum, s0, hs0, s1, hs1, cx, ch, gs, rs,
    sx1, rx1, sy1, ry1, sxl, rxl, syl, ryl, sx2, rx2, sy2, ry2, sx3, rx3, sy3, ry3,
    send_sem, recv_sem,
):
    nz, nx, ny = enth.shape
    top = OFF + nx
    gx, gy = lax.axis_index("gx"), lax.axis_index("gy")
    west, east = lax.rem(gx + ngx - 1, ngx), lax.rem(gx + 1, ngx)
    south, north = lax.rem(gy + ngy - 1, ngy), lax.rem(gy + 1, ngy)
    others = [(a, b) for a in (west, gx, east) for b in (south, gy, north) if not (a is gx and b is gy)]
    barrier = pltpu.get_barrier_semaphore()
    for other in others:
        pl.semaphore_signal(barrier, inc=1, device_id=other, device_id_type=pl.DeviceIdType.MESH)

    lane = lax.broadcasted_iota(jnp.int32, (1, ny), 1)
    own = slice(OFF, top)
    count = [0]

    def copy(src, dst, where):
        i = count[0]
        count[0] += 1
        c = pltpu.make_async_remote_copy(
            src_ref=src, dst_ref=dst, send_sem=send_sem.at[i], recv_sem=recv_sem.at[i],
            device_id=where, device_id_type=pl.DeviceIdType.MESH,
        )
        c.start()
        return c

    def send_x(sx, rx):
        return [
            copy(sx.at[LO], rx.at[HI], (west, gy)),
            copy(sx.at[HI], rx.at[LO], (east, gy)),
        ]

    def send_y(sy, ry):
        return [copy(sy, ry.at[HI], (gx, south)), copy(sy, ry.at[LO], (gx, north))]

    def send_y_corners(sy, ry):
        out = []
        for side, where in ((HI, south), (LO, north)):
            r = ry.at[side]
            out.append(copy(sy, r.at[:, 8 : 8 + nx], (gx, where)))
            out.append(copy(sy.at[:, 0:8], r.at[:, 8 + nx : 16 + nx], (west, where)))
            out.append(copy(sy.at[:, nx - 8 : nx], r.at[:, 0:8], (east, where)))
        return out

    def up(x, h, k=1):
        return pltpu.roll(jnp.where(lane < k, h, x), ny - k, 1)

    def down(x, h, k=1):
        return pltpu.roll(jnp.where(lane >= ny - k, h, x), k, 1)

    def pack(x, z, width, acc):
        group = ny // (2 * width)
        g = lax.rem(z, group)
        return jnp.where(lane // (2 * width) == g, pltpu.roll(x, g * (2 * width) + width, 1), acc)

    def unpack(packed, z, width):
        group = ny // (2 * width)
        g = lax.rem(z, group)
        return pltpu.roll(packed, ny - (g * (2 * width) + width), 1)

    def merged(from_lo, from_hi, width):
        return jnp.where(lane % (2 * width) >= width, from_hi, from_lo)

    def rows_of(ref, row):
        rows = ref.shape[1]
        return ref.reshape(ref.shape[0] * rows, ny), rows, row

    def get_row(ref, row, z0=0):
        flat, rows, row = rows_of(ref, row)
        return flat[pl.ds(z0 * rows + row, nz, stride=rows), :]

    def put_row(ref, row, value, z0=0):
        flat, rows, row = rows_of(ref, row)
        flat[pl.ds(z0 * rows + row, nz, stride=rows), :] = value

    def start(z, acc):
        accu, accs = acc
        e = enth[z] - LATENT_HEAT * phase[z].astype(F32)
        r = 1.0 / heat[z]
        t = e * r
        s = jnp.sqrt(cond[z])
        u = s * t
        ihc[z], tm[z], ex[z] = r, t, e
        sq[z, own], ua[z, own] = s, u
        return pack(u, z, 1, accu), pack(s, z, 1, accs)

    zero = jnp.zeros((nx, ny), F32)
    sy1[0], sy1[1] = loop(0, nz, start, (zero, zero), U_START)
    for i, ref in enumerate((ua, sq)):
        sx1[LO, i] = get_row(ref, OFF)
        sx1[HI, i] = get_row(ref, top - 1)
    pl.semaphore_wait(barrier, len(others))
    first = send_x(sx1, rx1) + send_y(sy1, ry1)

    def level_group(q, _):
        def one(g, acc):
            z = q * 16 + g
            x = level[z]
            lv[z + 3, own] = x
            return pack(x, z, 4, acc)

        syl[q] = loop(0, 16, one, zero, 16)
        return 0

    lax.fori_loop(0, nz // 16, level_group, 0)
    for k in range(3):
        sxl[LO, k] = get_row(lv, OFF + k, 3)
        sxl[HI, k] = get_row(lv, top - 3 + k, 3)
    levels = send_x(sxl, rxl) + send_y_corners(syl, ryl)

    def ends(ref, rows):
        for k in range(3):
            ref[k, rows] = ref[3, rows]
            ref[nz + 3 + k, rows] = ref[nz + 2, rows]

    ends(lv, own)

    def weno_z(z, _):
        for r in range(0, nx, chunk):
            at = slice(OFF + r, OFF + r + chunk)
            v = [lv[z + k, at] for k in range(7)]
            g, f = weno(*[v[k + 1] - v[k] for k in range(6)])
            gs[z, r : r + chunk], rs[z, r : r + chunk] = g, f
        return 0

    loop(0, nz, weno_z, 0, U_WENO)

    def around(ref, z, packed):
        x = ref[z, own]
        h = unpack(packed, z, 1)
        return (
            ref[jnp.maximum(z - 1, 0), own] + ref[jnp.minimum(z + 1, nz - 1), own]
            + (ref[z, OFF - 1 : top - 1] + ref[z, OFF + 1 : top + 1])
            + (up(x, h) + down(x, h))
        )

    for c in first:
        c.wait()
    for i, ref in enumerate((ua, sq)):
        put_row(ref, OFF - 1, rx1[LO, i])
        put_row(ref, top, rx1[HI, i])

    pu = merged(ry1[LO, 0], ry1[HI, 0], 1)
    ps = merged(ry1[LO, 1], ry1[HI, 1], 1)

    def substep1(z, acc):
        w = around(sq, z, ps)
        s = sq[z, own]
        e = ex[z] + DT_HEAT * (s * (around(ua, z, pu) - tm[z] * w))
        t = e * ihc[z]
        u = s * t
        wsum[z], ex[z], tm[z], ub[z, own] = w, e, t, u
        return pack(u, z, 1, acc)

    sy2[...] = loop(0, nz, substep1, zero, U_SUB)
    sx2[LO] = get_row(ub, OFF)
    sx2[HI] = get_row(ub, top - 1)
    second = send_x(sx2, rx2) + send_y(sy2, ry2)

    for c in levels:
        c.wait()
    for k in range(3):
        put_row(lv, OFF - 3 + k, rxl[LO, k], 3)
        put_row(lv, top + k, rxl[HI, k], 3)
    wide = slice(OFF - 8, top + 8)

    def level_halo(z, _):
        q = z // 16
        hl[z + 3, wide] = unpack(merged(ryl[LO, q], ryl[HI, q], 4), z, 4)
        return 0

    loop(0, nz, level_halo, 0, 8)
    ends(lv, wide)
    ends(hl, wide)

    def weno_xy(z, _):
        half = z // TILE
        masks = [jnp.where(flag[half, 0, j] == 1, -DT_LEVEL, 0.0) for j in range(ny // TILE)]
        mask = jnp.full((1, ny), masks[0])
        for j in range(1, ny // TILE):
            mask = jnp.where(lane >= j * TILE, masks[j], mask)
        for r in range(0, nx, chunk):
            a = OFF + r
            x = lv[z + 3, a : a + chunk]
            v = [x if k == 3 else lv[z + 3, a + k - 3 : a + k - 3 + chunk] for k in range(7)]
            g1, f1 = weno(*[v[k + 1] - v[k] for k in range(6)])
            h = hl[z + 3, a : a + chunk]
            v = [down(x, h, k) for k in (3, 2, 1)] + [x] + [up(x, h, k) for k in (1, 2, 3)]
            g2, f2 = weno(*[v[k + 1] - v[k] for k in range(6)])
            at = slice(r, r + chunk)
            gs[z, at] = mask * jnp.sqrt(gs[z, at] + g1 + g2 + 1e-06)
            rs[z, at] = mask * jnp.sqrt(rs[z, at] + f1 + f2 + 1e-06)
        return 0

    def coefs(out, oz, orow, main, side, z, a, rows):
        at = slice(a, a + rows)
        x, h = main[z + 3, at], side[z + 3, at]
        d0 = main[z + 4, at] - main[z + 2, at]
        d1 = main[z + 3, a + 1 : a + 1 + rows] - main[z + 3, a - 1 : a - 1 + rows]
        d2 = up(x, h) - down(x, h)
        d0, d1, d2 = d0 * d0, d1 * d1, d2 * d2
        total = d0 + d1 + d2
        inv = recip(4.0 + 3.0 * total)
        to = slice(orow, orow + rows)
        out[0, oz, to] = (4.0 + total) * inv
        out[1, oz, to] = d0 * inv
        out[2, oz, to] = d1 * inv
        out[3, oz, to] = d2 * inv

    def coefs_x(i, _):
        coefs(cx, i, 0, lv, hl, i - 1, OFF - 8, nx + 16)
        return 0

    def coefs_h(z, _):
        coefs(ch, z, 0, hl, lv, z, OFF, nx)
        return 0

    loop(0, nz // 2, weno_xy, 0, U_WENO)

    for c in second:
        c.wait()
    put_row(ub, OFF - 1, rx2[LO])
    put_row(ub, top, rx2[HI])

    pu2 = merged(ry2[LO], ry2[HI], 1)

    def substep2_group(q, _):
        def substep2(g, acc):
            z = q * 32 + g
            e = ex[z] + DT_HEAT * (sq[z, own] * (around(ub, z, pu2) - tm[z] * wsum[z]))
            eout[z] = e + LATENT_HEAT * phase[z].astype(F32)
            s = GROWTH_RATE * (MELT_POINT - e * ihc[z])
            s0[z, own] = s
            return pack(s, z, 2, acc)

        sy3[q] = loop(0, 32, substep2, zero, U_SUB)
        return 0

    lax.fori_loop(0, nz // 32, substep2_group, 0)
    for k in range(2):
        sx3[LO, k] = get_row(s0, OFF + k)
        sx3[HI, k] = get_row(s0, top - 2 + k)
    third = send_x(sx3, rx3) + send_y_corners(sy3, ry3)

    loop(nz // 2, nz, weno_xy, 0, U_WENO)
    loop(0, nz + 2, coefs_x, 0, U_COEF)
    loop(0, nz, coefs_h, 0, U_COEF)

    for c in third:
        c.wait()
    for k in range(2):
        put_row(s0, OFF - 2 + k, rx3[LO, k])
        put_row(s0, top + k, rx3[HI, k])

    def speed_halo(z, _):
        q = z // 32
        hs0[z, wide] = unpack(merged(ry3[LO, q], ry3[HI, q], 2), z, 2)
        return 0

    loop(0, nz, speed_halo, 0, 8)

    def clamp(z):
        return jnp.minimum(jnp.maximum(z, 0), nz - 1)

    def sweep(c, cz, crow, main, zb, zc, za, side, a, rows):
        at, to = slice(a, a + rows), slice(crow, crow + rows)
        x = main[zc, at]
        return (
            c[0, cz, to] * x
            + c[1, cz, to] * (main[zb, at] + main[za, at])
            + c[2, cz, to] * (main[zc, a - 1 : a - 1 + rows] + main[zc, a + 1 : a + 1 + rows])
            + c[3, cz, to] * (up(x, side) + down(x, side))
        )

    def sweep1_x(i, _):
        b, m, t = clamp(i - 2), clamp(i - 1), clamp(i)
        s1[i, wide] = sweep(cx, i, 0, s0, b, m, t, hs0[m, wide], OFF - 8, nx + 16)
        return 0

    loop(0, nz + 2, sweep1_x, 0, U_SWEEP)

    def sweep1_h(z, _):
        hs1[z] = sweep(ch, z, 0, hs0, clamp(z - 1), z, clamp(z + 1), s0[z, own], OFF, nx)
        return 0

    loop(0, nz, sweep1_h, 0, U_SWEEP)

    def last(z, _):
        s = sweep(cx, z + 1, 8, s1, z, z + 1, z + 2, hs1[z], OFF, nx)
        lout[z] = level[z] + s * jnp.where(s >= 0.0, gs[z], rs[z])
        return 0

    loop(0, nz, last, 0, U_LAST)


CHUNK = 16


def body(ngx, ngy, enthalpy, heat_cap, conductivity, phase, level_set, band_flag):
    nz, nx, ny = enthalpy.shape
    tall = nx + 2 * OFF

    def vmem(*shape):
        return pltpu.VMEM(shape, F32)

    copies = 4 + 8 + 4 + 8
    scratch = [
        vmem(nz + 6, tall, ny),
        vmem(nz + 6, tall, ny),
        vmem(nz, tall, ny),
        vmem(nz, tall, ny),
        vmem(nz, tall, ny),
        vmem(nz, nx, ny),
        vmem(nz, nx, ny),
        vmem(nz, nx, ny),
        vmem(nz, nx, ny),
        vmem(nz, tall, ny),
        vmem(nz, tall, ny),
        vmem(nz + 2, tall, ny),
        vmem(nz, nx, ny),
        vmem(4, nz + 2, nx + 16, ny),
        vmem(4, nz, nx, ny),
        vmem(nz, nx, ny),
        vmem(nz, nx, ny),
        vmem(2, 2, nz, ny), vmem(2, 2, nz, ny), vmem(2, nx, ny), vmem(2, 2, nx, ny),
        vmem(2, 3, nz, ny), vmem(2, 3, nz, ny), vmem(nz // 16, nx, ny), vmem(2, nz // 16, nx + 16, ny),
        vmem(2, nz, ny), vmem(2, nz, ny), vmem(nx, ny), vmem(2, nx, ny),
        vmem(2, 2, nz, ny), vmem(2, 2, nz, ny), vmem(nz // 32, nx, ny), vmem(2, nz // 32, nx + 16, ny),
        pltpu.SemaphoreType.DMA((copies,)),
        pltpu.SemaphoreType.DMA((copies,)),
    ]
    whole = pl.BlockSpec(memory_space=pltpu.VMEM)
    out = jax.ShapeDtypeStruct((nz, nx, ny), F32)
    return pl.pallas_call(
        functools.partial(kernel, ngx, ngy, CHUNK),
        out_shape=(out, out),
        in_specs=[pl.BlockSpec(memory_space=pltpu.SMEM)] + [whole] * 5,
        out_specs=(whole, whole),
        scratch_shapes=scratch,
        compiler_params=pltpu.CompilerParams(
            collective_id=0, has_side_effects=True, vmem_limit_bytes=60 * 1024 * 1024
        ),
    )(band_flag, enthalpy, heat_cap, conductivity, phase, level_set)


def solution(mesh):
    spec = P(None, "gx", "gy")
    return jax.shard_map(
        functools.partial(body, mesh.shape["gx"], mesh.shape["gy"]),
        mesh=mesh, in_specs=(spec,) * 6, out_specs=(spec, spec), check_vma=False,
    )
```
